32 devices in a mesh: ch: 16 (over z, x, core), ta: 2 (over y).
Axes of the slice: x: 2, y: 2, z: 4, core: 2. Of those that a mesh axis runs over, the one named last changes fastest.
Arguments:
- raw_strain: float32 [2048, 3072], P('ch', 'ta'), may hold values from -6 to 6
- band_index: int32 [2048], P('ch'), may hold values from 0 to 3
- filter_taps: float32 [4, 33], replicated, may hold values from -1 to 1
Outputs:
- correlation: float32 [2, 65, 2048, 128], P(None, None, ('ch', 'ta'))
The draws below stay inside these ranges and needn't reach their ends.
All inputs are finite; a program needn't handle non-finite values.
Results may differ from the reference program's by a relative error of at most 0.0037.
Values may be sent and summed in bfloat16 or wider, within the bound.
A program may use at most 64 MiB of HBM per device.

```python
import math
import jax
import jax.numpy as jnp
from jax import lax

CH_DEV = 128
HF = 16
TAPS = 33
NBANDS = 4
LAGH = 32
LAGS = 65
ROUNDS = 2
RH = 1536
CHANNELS = 2048
SAMPLES = 3072
N_CH = 16


def with_ends(entries, key, least, largest):
    place = [jax.random.randint(jax.random.fold_in(key, axis), (), 0, length) for axis, length in enumerate(entries.shape)]
    main_axis = entries.shape.index(max(entries.shape))
    next_to = place[:main_axis] + [(place[main_axis] + 1) % entries.shape[main_axis]] + place[main_axis + 1:]
    return entries.at[tuple(place)].set(least).at[tuple(next_to)].set(largest)


def steps_of(key, shape, pieces, low, high):
    def one(axis_at, parts):
        heights = jax.random.uniform(jax.random.fold_in(jax.random.fold_in(key, 6), axis_at), (parts,), jnp.float32, low / len(pieces), high / len(pieces))
        return jnp.repeat(jnp.exp(heights), shape[axis_at] // parts).reshape((-1,) + (1,) * (len(shape) - axis_at - 1))

    loudness = one(*pieces[0])
    for cut in pieces[1:]:
        loudness = loudness * one(*cut)
    return loudness


def scatter_about(own_key, shape, deviation, reach, shards=(), kind=jnp.bfloat16):
    array = deviation * jax.random.normal(own_key, shape, jnp.float32)
    if shards:
        array = array * steps_of(own_key, shape, shards, -0.22, 0.18)
    return jnp.clip(array, -reach, reach).astype(kind)


def setup_inputs(seed: int = 0) -> dict:
    key_list = jax.random.split(jax.random.key(seed), 4)
    return {
        "raw_strain": scatter_about(key_list[0], (CHANNELS, SAMPLES), 1.0, 6.0, ((0, 16), (1, 2)), jnp.float32),
        "band_index": with_ends(jax.random.randint(key_list[1], (CHANNELS,), 0, NBANDS), jax.random.fold_in(key_list[1], 1), 0, NBANDS - 1).astype(jnp.int32),
        "filter_taps": scatter_about(key_list[2], (NBANDS, TAPS), TAPS ** -0.5, 1.0, (), jnp.float32),
    }


def reference(raw_strain, band_index, filter_taps):
    coeffs = filter_taps[band_index]
    padded = jnp.pad(raw_strain, ((0, 0), (HF, HF)))
    filtered = jnp.zeros_like(raw_strain)
    for step in range(TAPS):
        filtered = filtered + coeffs[:, step:step + 1] * padded[:, step:step + SAMPLES]
    magnitude = jnp.abs(filtered)
    cumulative = jnp.concatenate([jnp.zeros((CHANNELS, 1), jnp.float32), jnp.cumsum(magnitude, axis=1)], axis=1)
    times = jnp.arange(SAMPLES, dtype=jnp.int32)
    upper = jnp.minimum(times + RH, SAMPLES - 1) + 1
    lower = jnp.maximum(times - RH, 0)
    window_sum = jnp.take(cumulative, upper, axis=1) - jnp.take(cumulative, lower, axis=1)
    counted = (upper - lower).astype(jnp.float32)
    level = window_sum / counted[None, :]
    normalized = (filtered / (level + 1e-06)).astype(jnp.bfloat16)
    values = normalized.astype(jnp.float32)
    blocks = values.reshape(N_CH, CH_DEV, SAMPLES)
    shifted_pad = jnp.pad(blocks, ((0, 0), (0, 0), (LAGH, LAGH)))
    scale = 1.0 / math.sqrt(SAMPLES)
    rounds_out = []
    for round_id in range(ROUNDS):
        offset = (round_id + 1) * (N_CH // 4)
        partner = jnp.roll(blocks, offset, axis=0)

        def one_lag(lag):
            start = (2 * LAGH - lag).astype(jnp.int32)
            moved = lax.dynamic_slice_in_dim(shifted_pad, start, SAMPLES, 2)
            return jnp.einsum('bit,bjt->bij', moved, partner).reshape(CHANNELS, CH_DEV) * scale
        rounds_out.append(lax.map(one_lag, jnp.arange(LAGS, dtype=jnp.int32)))
    return jnp.stack(rounds_out)
```

```python
import functools
import math

import jax
import jax.numpy as jnp
from jax import lax
from jax.experimental import pallas as pl
from jax.experimental.pallas import tpu as pltpu
from jax.sharding import PartitionSpec as P

HF = 16
TAPS = 33
NBANDS = 4
LAGH = 32
LAGS = 65
ROUNDS = 2
FINE = 16
SUBS = 2
PADK = 128
MESH = pl.DeviceIdType.MESH
F32 = jnp.float32
BF16 = jnp.bfloat16


def split(x):
    high = x.astype(BF16)
    return high, (x - high.astype(F32)).astype(BF16)


def dot(a, b):
    return jnp.dot(a, b, preferred_element_type=F32)


def kernel(n_ta, n_ch, rows, length, raw_ref, band_ref, taps_ref, out_ref,
           x, xe, f, pre, suf, nbuf, own, shifted, qbuf, pt, acc, w_hi, w_lo, tri,
           local_sem, raw_send, raw_recv, z_send, q_recv, y_send, out_sem):
    a = lax.axis_index("ta")
    c = lax.axis_index("ch")
    off = n_ch // 4
    up = lax.rem(c + off, n_ch)
    down = lax.rem(c + n_ch - off, n_ch)
    whole = n_ta * length
    block = n_ta * rows
    chunk = length // SUBS
    n_chunks = n_ta * SUBS
    others = range(1, n_ta)

    def peer(p):
        return lax.rem(a + p, n_ta)

    def source(p):
        return lax.rem(a + n_ta - p, n_ta)

    def rows_of(g):
        return pl.ds(pl.multiple_of(g * rows, rows), rows)

    barrier = pltpu.get_barrier_semaphore()
    for target in (up, down):
        pl.semaphore_signal(barrier, inc=1, device_id=(target, a), device_id_type=MESH)
    for p in others:
        pl.semaphore_signal(barrier, inc=1, device_id=(c, peer(p)), device_id_type=MESH)
    pl.semaphore_wait(barrier, 2 + len(others))

    raw_copies = []
    for p in others:
        copy = pltpu.make_async_remote_copy(
            src_ref=raw_ref.at[rows_of(peer(p))], dst_ref=x.at[rows_of(a)],
            send_sem=raw_send.at[p], recv_sem=raw_recv.at[p],
            device_id=(c, peer(p)), device_id_type=MESH)
        copy.start()
        raw_copies.append(copy)
    mine = pltpu.make_async_copy(raw_ref.at[rows_of(a)], x.at[rows_of(a)], local_sem)
    mine.start()

    used = 160
    lane = lax.broadcasted_iota(jnp.int32, (used, 128), 1)
    row = lax.broadcasted_iota(jnp.int32, (used, 128), 0)
    diff = row - lane
    for b in range(NBANDS):
        w = jnp.zeros((used, 128), F32)
        for k in range(TAPS):
            w = jnp.where(diff == k, taps_ref[b, k], w)
        high, low = split(w)
        cols = slice(b * 128, (b + 1) * 128)
        w_hi[0:used, cols] = high
        w_lo[0:used, cols] = low
        w_hi[used:256, cols] = jnp.zeros((256 - used, 128), BF16)
        w_lo[used:256, cols] = jnp.zeros((256 - used, 128), BF16)
    r256 = lax.broadcasted_iota(jnp.int32, (256, 256), 0)
    c256 = lax.broadcasted_iota(jnp.int32, (256, 256), 1)
    tri[:, 0:256] = jnp.where(r256 <= c256, 1.0, 0.0).astype(BF16)
    tri[:, 256:512] = jnp.where(r256 >= c256, 1.0, 0.0).astype(BF16)
    pt[0:2 * LAGH, :] = jnp.zeros((2 * LAGH, ROUNDS * block), BF16)
    pt[2 * LAGH + whole:, :] = jnp.zeros((pt.shape[0] - 2 * LAGH - whole, ROUNDS * block), BF16)
    own[:, whole:] = jnp.zeros((rows, PADK), F32)

    bands = jnp.concatenate([band_ref[rows_of(a), :]] * n_ta, axis=0)
    bands = jnp.broadcast_to(bands, (block, 128))

    mine.wait()
    for p in others:
        pltpu.make_async_remote_copy(
            src_ref=x.at[rows_of(source(p))], dst_ref=x.at[rows_of(source(p))],
            send_sem=raw_send.at[p], recv_sem=raw_recv.at[p],
            device_id=(c, source(p)), device_id_type=MESH).wait_recv()

    xe[:, 128:128 + length] = x[...]
    zeros = jnp.zeros((rows, 128), F32)
    for g in range(n_ta):
        here = slice(g * rows, (g + 1) * rows)
        xe[here, 0:128] = x[(g - 1) * rows:g * rows, length - 128:] if g > 0 else zeros
        xe[here, 128 + length:] = x[(g + 1) * rows:(g + 2) * rows, 0:128] if g < n_ta - 1 else zeros
    moved = pltpu.roll(xe[...], 128 + length + 128 - (128 - HF), 1)
    x_hi, x_lo = split(moved)
    for n in range(length // 128):
        lanes = slice(128 * n, 128 * n + 256)
        res = dot(x_hi[:, lanes], w_hi[...]) + (dot(x_lo[:, lanes], w_hi[...]) + dot(x_hi[:, lanes], w_lo[...]))
        picked = res[:, 0:128]
        for b in range(1, NBANDS):
            picked = jnp.where(bands == b, res[:, b * 128:(b + 1) * 128], picked)
        f[:, 128 * n:128 * (n + 1)] = picked

    n_sum = length // 256
    total = jnp.zeros((block, 1), F32)
    totals = []
    for m in range(n_sum):
        lanes = slice(256 * m, 256 * (m + 1))
        high, low = split(jnp.abs(f[:, lanes]))
        res = dot(high, tri[...]) + dot(low, tri[...])
        pre[:, lanes] = res[:, 0:256] + total
        suf[:, lanes] = res[:, 256:512]
        part = res[:, 255:256]
        totals.append(part)
        total = total + part
    behind = jnp.zeros((block, 1), F32)
    for m in reversed(range(n_sum)):
        lanes = slice(256 * m, 256 * (m + 1))
        if m < n_sum - 1:
            behind = behind + totals[m + 1]
            suf[:, lanes] = suf[:, lanes] + behind

    z_copies = []
    for k in range(n_chunks):
        g, s = k // SUBS, k % SUBS
        lanes = slice(s * chunk, (s + 1) * chunk)
        here = slice(g * rows, (g + 1) * rows)
        window = jnp.broadcast_to(total[here], (rows, chunk))
        if g > 0:
            window = window + suf[(g - 1) * rows:g * rows, lanes]
        if g < n_ta - 1:
            window = window + pre[(g + 1) * rows:(g + 2) * rows, lanes]
        time = k * chunk + lax.broadcasted_iota(jnp.int32, (1, chunk), 1)
        counted = jnp.minimum(time + length, whole - 1) + 1 - jnp.maximum(time - length, 0)
        level = window * (1.0 / counted.astype(F32))
        normalized = (f[here, lanes] / (level + 1e-6)).astype(BF16)
        nbuf[k] = normalized
        own[:, k * chunk:(k + 1) * chunk] = normalized.astype(F32)
        copy = pltpu.make_async_remote_copy(
            src_ref=nbuf.at[k], dst_ref=qbuf.at[0, k, rows_of(a)],
            send_sem=z_send.at[0, k], recv_sem=q_recv.at[0, k, 0],
            device_id=(up, a), device_id_type=MESH)
        copy.start()
        z_copies.append(copy)

    step = min(rows, 16)
    for i in range(rows // step):
        part = own[i * step:(i + 1) * step, :]
        for fine in range(FINE):
            shifted[fine * rows + i * step:fine * rows + (i + 1) * step, :] = (
                pltpu.roll(part, LAGH + fine, 1).astype(BF16))

    y_copies = []

    def arrived(r, k, p):
        slot = qbuf.at[r, k, rows_of(source(p))]
        pltpu.make_async_remote_copy(
            src_ref=slot, dst_ref=slot, send_sem=z_send.at[0, k], recv_sem=q_recv.at[r, k, p],
            device_id=(c, a), device_id_type=MESH).wait_recv()

    def forward(r, k):
        arrived(r, k, 0)
        slot = (r, k, rows_of(a))
        if r + 1 < ROUNDS:
            copy = pltpu.make_async_remote_copy(
                src_ref=qbuf.at[slot], dst_ref=qbuf.at[r + 1, k, rows_of(a)],
                send_sem=z_send.at[r + 1, k], recv_sem=q_recv.at[r + 1, k, 0],
                device_id=(up, a), device_id_type=MESH)
            copy.start()
            z_copies.append(copy)
        for p in others:
            copy = pltpu.make_async_remote_copy(
                src_ref=qbuf.at[slot], dst_ref=qbuf.at[slot],
                send_sem=y_send.at[r, k, p], recv_sem=q_recv.at[r, k, p],
                device_id=(c, peer(p)), device_id_type=MESH)
            copy.start()
            y_copies.append(copy)

    scale = 1.0 / math.sqrt(whole)
    half = FINE // 2
    coarse = LAGS // FINE

    def correlate(k):
        for r in range(ROUNDS):
            for p in others:
                arrived(r, k, p)
            pt[2 * LAGH + k * chunk:2 * LAGH + (k + 1) * chunk, r * block:(r + 1) * block] = qbuf[r, k].T
        first, last = k == 0, k == n_chunks - 1
        begin = k * chunk
        depth = chunk + (PADK if last else 0)

        def piece(lag0, n_lags, row0, shift):
            res = dot(shifted[pl.ds(row0, n_lags * rows), begin:begin + depth],
                      pt[pl.ds(begin + shift, depth), :])
            for r in range(ROUNDS):
                part = res[:, r * block:(r + 1) * block].reshape(n_lags, rows, block)
                where = (r, pl.ds(lag0, n_lags))
                if not first:
                    part = acc[where] + part
                acc[where] = part * scale if last else part

        def send(lag0, n_lags, slot):
            return pltpu.make_async_copy(
                acc.at[:, pl.ds(lag0, n_lags)], out_ref.at[:, pl.ds(lag0, n_lags)], out_sem.at[slot])

        def body(i, carry):
            b, h = i // 2, i % 2
            piece(i * half, half, pl.multiple_of(h * (half * rows), half * rows),
                  pl.multiple_of(b * FINE, FINE))
            if last:
                send(i * half, half, i).start()
            return carry

        lax.fori_loop(0, 2 * coarse, body, 0)
        piece(coarse * FINE, 1, 0, coarse * FINE)
        if last:
            send(coarse * FINE, 1, 2 * coarse).start()
            for i in range(2 * coarse):
                send(i * half, half, i).wait()
            send(coarse * FINE, 1, 2 * coarse).wait()

    for turn in range(n_chunks + 2):
        if turn < n_chunks:
            forward(0, turn)
        if 0 <= turn - 1 < n_chunks:
            forward(1, turn - 1)
        if turn - 2 >= 0:
            correlate(turn - 2)

    for copy in raw_copies + z_copies + y_copies:
        copy.wait_send()


def on_device(n_ta, n_ch, raw_strain, band_index, filter_taps):
    block, length = raw_strain.shape
    rows = block // n_ta
    whole = n_ta * length
    chunk = length // SUBS
    n_chunks = n_ta * SUBS
    dma = pltpu.SemaphoreType.DMA
    return pl.pallas_call(
        functools.partial(kernel, n_ta, n_ch, rows, length),
        out_shape=jax.ShapeDtypeStruct((ROUNDS, LAGS, rows, block), F32),
        in_specs=[
            pl.BlockSpec(memory_space=pl.ANY),
            pl.BlockSpec(memory_space=pltpu.VMEM),
            pl.BlockSpec(memory_space=pltpu.SMEM),
        ],
        out_specs=pl.BlockSpec(memory_space=pl.ANY),
        scratch_shapes=[
            pltpu.VMEM((block, length), F32),
            pltpu.VMEM((block, length + 256), F32),
            pltpu.VMEM((block, length), F32),
            pltpu.VMEM((block, length), F32),
            pltpu.VMEM((block, length), F32),
            pltpu.VMEM((n_chunks, rows, chunk), BF16),
            pltpu.VMEM((rows, whole + PADK), F32),
            pltpu.VMEM((FINE * rows, whole + PADK), BF16),
            pltpu.VMEM((ROUNDS, n_chunks, block, chunk), BF16),
            pltpu.VMEM((2 * LAGH + whole + PADK, ROUNDS * block), BF16),
            pltpu.VMEM((ROUNDS, LAGS, rows, block), F32),
            pltpu.VMEM((256, NBANDS * 128), BF16),
            pltpu.VMEM((256, NBANDS * 128), BF16),
            pltpu.VMEM((256, 512), BF16),
            dma(()),
            dma((n_ta,)),
            dma((n_ta,)),
            dma((ROUNDS, n_chunks)),
            dma((ROUNDS, n_chunks, n_ta)),
            dma((ROUNDS, n_chunks, n_ta)),
            dma((2 * (LAGS // FINE) + 1,)),
        ],
        compiler_params=pltpu.CompilerParams(
            collective_id=0, has_side_effects=True, vmem_limit_bytes=56 * 1024 * 1024),
    )(raw_strain, band_index.reshape(block, 1), filter_taps)


def solution(mesh):
    placed = (P("ch", "ta"), P("ch"), P())
    return jax.shard_map(
        functools.partial(on_device, mesh.shape["ta"], mesh.shape["ch"]),
        mesh=mesh,
        in_specs=placed,
        out_specs=P(None, None, ("ch", "ta"), None),
        check_vma=False,
    )
```

```python
import functools
import math

import jax
import jax.numpy as jnp
from jax import lax
from jax.experimental import pallas as pl
from jax.experimental.pallas import tpu as pltpu
from jax.sharding import PartitionSpec as P

HF = 16
TAPS = 33
NBANDS = 4
LAGH = 32
LAGS = 65
ROUNDS = 2
FINE = 16
SUBS = 2
PADK = 128
MESH = pl.DeviceIdType.MESH
F32 = jnp.float32
BF16 = jnp.bfloat16


def split(x):
    high = x.astype(BF16)
    return high, (x - high.astype(F32)).astype(BF16)


def dot(a, b):
    return jnp.dot(a, b, preferred_element_type=F32)


def kernel(n_ta, n_ch, rows, length, raw_ref, band_ref, taps_ref, out_ref,
           x, xe, f, pre, suf, nbuf, own, shifted, qbuf, pt, acc, w_hi, w_lo, tri, xs_hi, xs_lo,
           local_sem, raw_send, raw_recv, z_send, q_recv, y_send, out_sem):
    a = lax.axis_index("ta")
    c = lax.axis_index("ch")
    off = n_ch // 4
    up = lax.rem(c + off, n_ch)
    down = lax.rem(c + n_ch - off, n_ch)
    whole = n_ta * length
    block = n_ta * rows
    chunk = length // SUBS
    n_chunks = n_ta * SUBS
    others = range(1, n_ta)

    def peer(p):
        return lax.rem(a + p, n_ta)

    def source(p):
        return lax.rem(a + n_ta - p, n_ta)

    def rows_of(g):
        return pl.ds(pl.multiple_of(g * rows, rows), rows)

    barrier = pltpu.get_barrier_semaphore()
    for target in (up, down):
        pl.semaphore_signal(barrier, inc=1, device_id=(target, a), device_id_type=MESH)
    for p in others:
        pl.semaphore_signal(barrier, inc=1, device_id=(c, peer(p)), device_id_type=MESH)
    pl.semaphore_wait(barrier, 2 + len(others))

    raw_copies = []
    for p in others:
        copy = pltpu.make_async_remote_copy(
            src_ref=raw_ref.at[rows_of(peer(p))], dst_ref=x.at[rows_of(a)],
            send_sem=raw_send.at[p], recv_sem=raw_recv.at[p],
            device_id=(c, peer(p)), device_id_type=MESH)
        copy.start()
        raw_copies.append(copy)
    mine = pltpu.make_async_copy(raw_ref.at[rows_of(a)], x.at[rows_of(a)], local_sem)
    mine.start()

    used = 160
    lane = lax.broadcasted_iota(jnp.int32, (used, 128), 1)
    row = lax.broadcasted_iota(jnp.int32, (used, 128), 0)
    diff = row - lane
    for b in range(NBANDS):
        w = jnp.zeros((used, 128), F32)
        for k in range(TAPS):
            w = jnp.where(diff == k, taps_ref[b, k], w)
        high, low = split(w)
        cols = slice(b * 128, (b + 1) * 128)
        w_hi[0:used, cols] = high
        w_lo[0:used, cols] = low
        w_hi[used:256, cols] = jnp.zeros((256 - used, 128), BF16)
        w_lo[used:256, cols] = jnp.zeros((256 - used, 128), BF16)
    r256 = lax.broadcasted_iota(jnp.int32, (256, 256), 0)
    c256 = lax.broadcasted_iota(jnp.int32, (256, 256), 1)
    tri[:, 0:256] = jnp.where(r256 <= c256, 1.0, 0.0).astype(BF16)
    tri[:, 256:512] = jnp.where(r256 >= c256, 1.0, 0.0).astype(BF16)
    pt[0:2 * LAGH, :] = jnp.zeros((2 * LAGH, ROUNDS * block), BF16)
    pt[2 * LAGH + whole:, :] = jnp.zeros((pt.shape[0] - 2 * LAGH - whole, ROUNDS * block), BF16)
    own[:, whole:] = jnp.zeros((rows, PADK), BF16)

    row = lax.broadcasted_iota(jnp.int32, (block, block), 0)
    chosen = lax.broadcasted_iota(jnp.int32, (block, block), 1) == a * rows + lax.rem(row, rows)
    bands = jnp.sum(jnp.where(chosen, band_ref[...].astype(F32), 0.0), axis=1, keepdims=True)
    bands = jnp.broadcast_to(bands, (block, 128))

    mine.wait()
    for p in others:
        pltpu.make_async_remote_copy(
            src_ref=x.at[rows_of(source(p))], dst_ref=x.at[rows_of(source(p))],
            send_sem=raw_send.at[p], recv_sem=raw_recv.at[p],
            device_id=(c, source(p)), device_id_type=MESH).wait_recv()

    xe[:, 128:128 + length] = x[...]
    zeros = jnp.zeros((rows, 128), F32)
    for g in range(n_ta):
        here = slice(g * rows, (g + 1) * rows)
        xe[here, 0:128] = x[(g - 1) * rows:g * rows, length - 128:] if g > 0 else zeros
        xe[here, 128 + length:] = x[(g + 1) * rows:(g + 2) * rows, 0:128] if g < n_ta - 1 else zeros
    moved = pltpu.roll(xe[...], 128 + length + 128 - (128 - HF), 1)
    x_hi, x_lo = split(moved)
    for n in range(length // 128):
        lanes = slice(128 * n, 128 * n + 256)
        xs_hi[n * block:(n + 1) * block, :] = x_hi[:, lanes]
        xs_lo[n * block:(n + 1) * block, :] = x_lo[:, lanes]
    for m in range(length // 512):
        part = slice(4 * m * block, 4 * (m + 1) * block)
        res = dot(xs_hi[part, :], w_hi[...]) + (dot(xs_lo[part, :], w_hi[...]) + dot(xs_hi[part, :], w_lo[...]))
        for q in range(4):
            one = res[q * block:(q + 1) * block]
            picked = one[:, 0:128]
            for b in range(1, NBANDS):
                picked = jnp.where(bands == float(b), one[:, b * 128:(b + 1) * 128], picked)
            f[:, 128 * (4 * m + q):128 * (4 * m + q + 1)] = picked

    n_sum = length // 256
    total = jnp.zeros((block, 1), F32)
    totals = []
    for m in range(n_sum):
        lanes = slice(256 * m, 256 * (m + 1))
        high, low = split(jnp.abs(f[:, lanes]))
        res = dot(high, tri[...]) + dot(low, tri[...])
        pre[:, lanes] = res[:, 0:256] + total
        suf[:, lanes] = res[:, 256:512]
        part = res[:, 255:256]
        totals.append(part)
        total = total + part
    behind = jnp.zeros((block, 1), F32)
    for m in reversed(range(n_sum)):
        lanes = slice(256 * m, 256 * (m + 1))
        if m < n_sum - 1:
            behind = behind + totals[m + 1]
            suf[:, lanes] = suf[:, lanes] + behind

    z_copies = []
    for k in range(n_chunks):
        g, s = k // SUBS, k % SUBS
        lanes = slice(s * chunk, (s + 1) * chunk)
        here = slice(g * rows, (g + 1) * rows)
        window = jnp.broadcast_to(total[here], (rows, chunk))
        if g > 0:
            window = window + suf[(g - 1) * rows:g * rows, lanes]
        if g < n_ta - 1:
            window = window + pre[(g + 1) * rows:(g + 2) * rows, lanes]
        time = k * chunk + lax.broadcasted_iota(jnp.int32, (1, chunk), 1)
        counted = jnp.minimum(time + length, whole - 1) + 1 - jnp.maximum(time - length, 0)
        level = window * (1.0 / counted.astype(F32))
        normalized = (f[here, lanes] / (level + 1e-6)).astype(BF16)
        nbuf[k] = normalized
        own[:, k * chunk:(k + 1) * chunk] = normalized
        copy = pltpu.make_async_remote_copy(
            src_ref=nbuf.at[k], dst_ref=qbuf.at[0, k, rows_of(a)],
            send_sem=z_send.at[0, k], recv_sem=q_recv.at[0, k, 0],
            device_id=(up, a), device_id_type=MESH)
        copy.start()
        z_copies.append(copy)

    step = min(rows, 16)
    n_parts = rows // step

    def shift_part(i):
        part = own[i * step:(i + 1) * step, :]
        for fine in range(FINE):
            shifted[fine * rows + i * step:fine * rows + (i + 1) * step, :] = (
                pltpu.roll(part, LAGH + fine, 1).astype(BF16))

    y_copies = []

    def arrived(r, k, p):
        slot = qbuf.at[r, k, rows_of(source(p))]
        pltpu.make_async_remote_copy(
            src_ref=slot, dst_ref=slot, send_sem=z_send.at[0, k], recv_sem=q_recv.at[r, k, p],
            device_id=(c, a), device_id_type=MESH).wait_recv()

    def forward(r, k):
        arrived(r, k, 0)
        slot = (r, k, rows_of(a))
        if r + 1 < ROUNDS:
            copy = pltpu.make_async_remote_copy(
                src_ref=qbuf.at[slot], dst_ref=qbuf.at[r + 1, k, rows_of(a)],
                send_sem=z_send.at[r + 1, k], recv_sem=q_recv.at[r + 1, k, 0],
                device_id=(up, a), device_id_type=MESH)
            copy.start()
            z_copies.append(copy)
        for p in others:
            copy = pltpu.make_async_remote_copy(
                src_ref=qbuf.at[slot], dst_ref=qbuf.at[slot],
                send_sem=y_send.at[r, k, p], recv_sem=q_recv.at[r, k, p],
                device_id=(c, peer(p)), device_id_type=MESH)
            copy.start()
            y_copies.append(copy)

    scale = 1.0 / math.sqrt(whole)
    half = FINE // 2
    coarse = LAGS // FINE

    def correlate(k):
        for r in range(ROUNDS):
            for p in others:
                arrived(r, k, p)
            pt[2 * LAGH + k * chunk:2 * LAGH + (k + 1) * chunk, r * block:(r + 1) * block] = qbuf[r, k].T
        first, last = k == 0, k == n_chunks - 1
        begin = k * chunk
        depth = chunk + (PADK if last else 0)

        def piece(lag0, n_lags, row0, shift):
            res = dot(shifted[pl.ds(row0, n_lags * rows), begin:begin + depth],
                      pt[pl.ds(begin + shift, depth), :])
            for r in range(ROUNDS):
                part = res[:, r * block:(r + 1) * block].reshape(n_lags, rows, block)
                where = (r, pl.ds(lag0, n_lags))
                if not first:
                    part = acc[where] + part
                acc[where] = part * scale if last else part

        def send(lag0, n_lags, slot):
            return pltpu.make_async_copy(
                acc.at[:, pl.ds(lag0, n_lags)], out_ref.at[:, pl.ds(lag0, n_lags)], out_sem.at[slot])

        def body(i, carry):
            b, h = i // 2, i % 2
            piece(i * half, half, pl.multiple_of(h * (half * rows), half * rows),
                  pl.multiple_of(b * FINE, FINE))
            if last:
                send(i * half, half, i).start()
            return carry

        lax.fori_loop(0, 2 * coarse, body, 0)
        piece(coarse * FINE, 1, 0, coarse * FINE)
        if last:
            send(coarse * FINE, 1, 2 * coarse).start()
            for i in range(2 * coarse):
                send(i * half, half, i).wait()
            send(coarse * FINE, 1, 2 * coarse).wait()

    delay = max(2, n_parts - 1)
    shift_part(0)
    for turn in range(n_chunks + delay):
        if turn < n_chunks:
            forward(0, turn)
        if 0 <= turn - 1 < n_chunks:
            forward(1, turn - 1)
        if turn + 1 < n_parts:
            shift_part(turn + 1)
        if turn - delay >= 0:
            correlate(turn - delay)

    for copy in raw_copies + z_copies + y_copies:
        copy.wait_send()


def on_device(n_ta, n_ch, raw_strain, band_index, filter_taps):
    block, length = raw_strain.shape
    rows = block // n_ta
    whole = n_ta * length
    chunk = length // SUBS
    n_chunks = n_ta * SUBS
    dma = pltpu.SemaphoreType.DMA
    return pl.pallas_call(
        functools.partial(kernel, n_ta, n_ch, rows, length),
        out_shape=jax.ShapeDtypeStruct((ROUNDS, LAGS, rows, block), F32),
        in_specs=[
            pl.BlockSpec(memory_space=pl.ANY),
            pl.BlockSpec(memory_space=pltpu.VMEM),
            pl.BlockSpec(memory_space=pltpu.SMEM),
        ],
        out_specs=pl.BlockSpec(memory_space=pl.ANY),
        scratch_shapes=[
            pltpu.VMEM((block, length), F32),
            pltpu.VMEM((block, length + 256), F32),
            pltpu.VMEM((block, length), F32),
            pltpu.VMEM((block, length), F32),
            pltpu.VMEM((block, length), F32),
            pltpu.VMEM((n_chunks, rows, chunk), BF16),
            pltpu.VMEM((rows, whole + PADK), BF16),
            pltpu.VMEM((FINE * rows, whole + PADK), BF16),
            pltpu.VMEM((ROUNDS, n_chunks, block, chunk), BF16),
            pltpu.VMEM((2 * LAGH + whole + PADK, ROUNDS * block), BF16),
            pltpu.VMEM((ROUNDS, LAGS, rows, block), F32),
            pltpu.VMEM((256, NBANDS * 128), BF16),
            pltpu.VMEM((256, NBANDS * 128), BF16),
            pltpu.VMEM((256, 512), BF16),
            pltpu.VMEM((length // 128 * block, 256), BF16),
            pltpu.VMEM((length // 128 * block, 256), BF16),
            dma(()),
            dma((n_ta,)),
            dma((n_ta,)),
            dma((ROUNDS, n_chunks)),
            dma((ROUNDS, n_chunks, n_ta)),
            dma((ROUNDS, n_chunks, n_ta)),
            dma((2 * (LAGS // FINE) + 1,)),
        ],
        compiler_params=pltpu.CompilerParams(
            collective_id=0, has_side_effects=True, vmem_limit_bytes=32 * 1024 * 1024),
    )(raw_strain, band_index.reshape(1, block), filter_taps)


def solution(mesh):
    placed = (P("ch", "ta"), P("ch"), P())
    return jax.shard_map(
        functools.partial(on_device, mesh.shape["ta"], mesh.shape["ch"]),
        mesh=mesh,
        in_specs=placed,
        out_specs=P(None, None, ("ch", "ta"), None),
        check_vma=False,
    )
```

```python
import functools
import math

import jax
import jax.numpy as jnp
from jax import lax
from jax.experimental import pallas as pl
from jax.experimental.pallas import tpu as pltpu
from jax.sharding import PartitionSpec as P

HF = 16
TAPS = 33
NBANDS = 4
LAGH = 32
LAGS = 65
ROUNDS = 2
FINE = 16
SUBS = 2
PARTS = 2
PADK = 128
MESH = pl.DeviceIdType.MESH
F32 = jnp.float32
BF16 = jnp.bfloat16


def split(x):
    high = x.astype(BF16)
    return high, (x - high.astype(F32)).astype(BF16)


def dot(a, b):
    return jnp.dot(a, b, preferred_element_type=F32)


def kernel(n_ta, n_ch, rows, length, n_parts, raw_ref, band_hbm, taps_hbm, out_ref,
           band_ref, taps_ref, x, xe, f, pre, suf, nbuf, own, shifted, qbuf, pt, acc, w_hi, w_lo, tri, xs_hi, xs_lo,
           small_sem, local_sem, raw_send, raw_recv, z_send, q_recv, y_send, out_sem):
    a = lax.axis_index("ta")
    c = lax.axis_index("ch")
    off = n_ch // 4
    up = lax.rem(c + off, n_ch)
    down = lax.rem(c + n_ch - off, n_ch)
    whole = n_ta * length
    block = n_ta * rows
    hr = rows // n_parts
    tall = n_ta * hr
    chunk = length // SUBS
    n_chunks = n_ta * SUBS
    others = range(1, n_ta)

    def peer(p):
        return lax.rem(a + p, n_ta)

    def source(p):
        return lax.rem(a + n_ta - p, n_ta)

    def rows_of(g, h):
        return pl.ds(pl.multiple_of(g * rows + h * hr, hr), hr)

    def place(g):
        return pl.ds(pl.multiple_of(g * hr, hr), hr)

    small = [pltpu.make_async_copy(band_hbm, band_ref, small_sem.at[0]),
             pltpu.make_async_copy(taps_hbm, taps_ref, small_sem.at[1])]
    mine = [pltpu.make_async_copy(raw_ref.at[rows_of(a, h)], x.at[h, place(a)], local_sem.at[h])
            for h in range(n_parts)]
    for copy in small + mine:
        copy.start()

    barrier = pltpu.get_barrier_semaphore()
    for target in (up, down):
        pl.semaphore_signal(barrier, inc=1, device_id=(target, a), device_id_type=MESH)
    for p in others:
        pl.semaphore_signal(barrier, inc=1, device_id=(c, peer(p)), device_id_type=MESH)
    pl.semaphore_wait(barrier, 2 + len(others))

    raw_copies = []
    for h in range(n_parts):
        for p in others:
            copy = pltpu.make_async_remote_copy(
                src_ref=raw_ref.at[rows_of(peer(p), h)], dst_ref=x.at[h, place(a)],
                send_sem=raw_send.at[h, p], recv_sem=raw_recv.at[h, p],
                device_id=(c, peer(p)), device_id_type=MESH)
            copy.start()
            raw_copies.append(copy)
    for copy in small:
        copy.wait()

    used = 160
    lane = lax.broadcasted_iota(jnp.int32, (used, 128), 1)
    row = lax.broadcasted_iota(jnp.int32, (used, 128), 0)
    diff = row - lane
    for b in range(NBANDS):
        w = jnp.zeros((used, 128), F32)
        for k in range(TAPS):
            w = jnp.where(diff == k, taps_ref[b, k], w)
        high, low = split(w)
        cols = slice(b * 128, (b + 1) * 128)
        w_hi[0:used, cols] = high
        w_lo[0:used, cols] = low
        w_hi[used:256, cols] = jnp.zeros((256 - used, 128), BF16)
        w_lo[used:256, cols] = jnp.zeros((256 - used, 128), BF16)
    r256 = lax.broadcasted_iota(jnp.int32, (256, 256), 0)
    c256 = lax.broadcasted_iota(jnp.int32, (256, 256), 1)
    tri[:, 0:256] = jnp.where(r256 <= c256, 1.0, 0.0).astype(BF16)
    tri[:, 256:512] = jnp.where(r256 >= c256, 1.0, 0.0).astype(BF16)
    pt[0:2 * LAGH, :] = jnp.zeros((2 * LAGH, ROUNDS * block), BF16)
    pt[2 * LAGH + whole:, :] = jnp.zeros((pt.shape[0] - 2 * LAGH - whole, ROUNDS * block), BF16)
    own[:, whole:] = jnp.zeros((rows, PADK), BF16)

    z_copies = []

    def prepare(h):
        row = lax.broadcasted_iota(jnp.int32, (tall, block), 0)
        chosen = lax.broadcasted_iota(jnp.int32, (tall, block), 1) == a * rows + h * hr + lax.rem(row, hr)
        bands = jnp.sum(jnp.where(chosen, band_ref[...].astype(F32), 0.0), axis=1, keepdims=True)
        bands = jnp.broadcast_to(bands, (tall, 128))

        mine[h].wait()
        for p in others:
            slot = x.at[h, place(source(p))]
            pltpu.make_async_remote_copy(
                src_ref=slot, dst_ref=slot,
                send_sem=raw_send.at[h, p], recv_sem=raw_recv.at[h, p],
                device_id=(c, source(p)), device_id_type=MESH).wait_recv()

        xe[:, 128:128 + length] = x[h]
        zeros = jnp.zeros((hr, 128), F32)
        for g in range(n_ta):
            here = slice(g * hr, (g + 1) * hr)
            xe[here, 0:128] = x[h, (g - 1) * hr:g * hr, length - 128:] if g > 0 else zeros
            xe[here, 128 + length:] = x[h, (g + 1) * hr:(g + 2) * hr, 0:128] if g < n_ta - 1 else zeros
        moved = pltpu.roll(xe[...], 128 + length + 128 - (128 - HF), 1)
        x_hi, x_lo = split(moved)
        for n in range(length // 128):
            lanes = slice(128 * n, 128 * n + 256)
            xs_hi[n * tall:(n + 1) * tall, :] = x_hi[:, lanes]
            xs_lo[n * tall:(n + 1) * tall, :] = x_lo[:, lanes]
        for m in range(length // 512):
            part = slice(4 * m * tall, 4 * (m + 1) * tall)
            res = dot(xs_hi[part, :], w_hi[...]) + (dot(xs_lo[part, :], w_hi[...]) + dot(xs_hi[part, :], w_lo[...]))
            for q in range(4):
                one = res[q * tall:(q + 1) * tall]
                picked = one[:, 0:128]
                for b in range(1, NBANDS):
                    picked = jnp.where(bands == float(b), one[:, b * 128:(b + 1) * 128], picked)
                f[:, 128 * (4 * m + q):128 * (4 * m + q + 1)] = picked

        n_sum = length // 256
        total = jnp.zeros((tall, 1), F32)
        totals = []
        for m in range(n_sum):
            lanes = slice(256 * m, 256 * (m + 1))
            high, low = split(jnp.abs(f[:, lanes]))
            res = dot(high, tri[...]) + dot(low, tri[...])
            pre[:, lanes] = res[:, 0:256] + total
            suf[:, lanes] = res[:, 256:512]
            part = res[:, 255:256]
            totals.append(part)
            total = total + part
        behind = jnp.zeros((tall, 1), F32)
        for m in reversed(range(n_sum)):
            lanes = slice(256 * m, 256 * (m + 1))
            if m < n_sum - 1:
                behind = behind + totals[m + 1]
                suf[:, lanes] = suf[:, lanes] + behind

        ours = slice(h * hr, (h + 1) * hr)
        for k in range(n_chunks):
            g, s = k // SUBS, k % SUBS
            lanes = slice(s * chunk, (s + 1) * chunk)
            here = slice(g * hr, (g + 1) * hr)
            window = jnp.broadcast_to(total[here], (hr, chunk))
            if g > 0:
                window = window + suf[(g - 1) * hr:g * hr, lanes]
            if g < n_ta - 1:
                window = window + pre[(g + 1) * hr:(g + 2) * hr, lanes]
            time = k * chunk + lax.broadcasted_iota(jnp.int32, (1, chunk), 1)
            counted = jnp.minimum(time + length, whole - 1) + 1 - jnp.maximum(time - length, 0)
            level = window * (1.0 / counted.astype(F32))
            normalized = (f[here, lanes] / (level + 1e-6)).astype(BF16)
            nbuf[k, ours] = normalized
            own[ours, k * chunk:(k + 1) * chunk] = normalized
            copy = pltpu.make_async_remote_copy(
                src_ref=nbuf.at[k, ours], dst_ref=qbuf.at[0, k, rows_of(a, h)],
                send_sem=z_send.at[0, k, h], recv_sem=q_recv.at[0, k, h, 0],
                device_id=(up, a), device_id_type=MESH)
            copy.start()
            z_copies.append(copy)

    step = min(rows, 16)
    n_shift = rows // step

    def shift_part(i):
        part = own[i * step:(i + 1) * step, :]
        for fine in range(FINE):
            shifted[fine * rows + i * step:fine * rows + (i + 1) * step, :] = (
                pltpu.roll(part, LAGH + fine, 1).astype(BF16))

    y_copies = []

    def arrived(r, k, h, p):
        slot = qbuf.at[r, k, rows_of(source(p), h)]
        pltpu.make_async_remote_copy(
            src_ref=slot, dst_ref=slot, send_sem=z_send.at[0, k, h], recv_sem=q_recv.at[r, k, h, p],
            device_id=(c, a), device_id_type=MESH).wait_recv()

    def forward(r, k, h):
        arrived(r, k, h, 0)
        slot = (r, k, rows_of(a, h))
        if r + 1 < ROUNDS:
            copy = pltpu.make_async_remote_copy(
                src_ref=qbuf.at[slot], dst_ref=qbuf.at[r + 1, k, rows_of(a, h)],
                send_sem=z_send.at[r + 1, k, h], recv_sem=q_recv.at[r + 1, k, h, 0],
                device_id=(up, a), device_id_type=MESH)
            copy.start()
            z_copies.append(copy)
        for p in others:
            copy = pltpu.make_async_remote_copy(
                src_ref=qbuf.at[slot], dst_ref=qbuf.at[slot],
                send_sem=y_send.at[r, k, h, p], recv_sem=q_recv.at[r, k, h, p],
                device_id=(c, peer(p)), device_id_type=MESH)
            copy.start()
            y_copies.append(copy)

    scale = 1.0 / math.sqrt(whole)
    half = FINE // 2
    coarse = LAGS // FINE

    def correlate(k):
        for r in range(ROUNDS):
            for h in range(n_parts):
                for p in others:
                    arrived(r, k, h, p)
            pt[2 * LAGH + k * chunk:2 * LAGH + (k + 1) * chunk, r * block:(r + 1) * block] = qbuf[r, k].T
        first, last = k == 0, k == n_chunks - 1
        begin = k * chunk
        depth = chunk + (PADK if last else 0)

        def piece(lag0, n_lags, row0, shift):
            res = dot(shifted[pl.ds(row0, n_lags * rows), begin:begin + depth],
                      pt[pl.ds(begin + shift, depth), :])
            for r in range(ROUNDS):
                part = res[:, r * block:(r + 1) * block].reshape(n_lags, rows, block)
                where = (r, pl.ds(lag0, n_lags))
                if not first:
                    part = acc[where] + part
                acc[where] = part * scale if last else part

        def send(lag0, n_lags, slot):
            return pltpu.make_async_copy(
                acc.at[:, pl.ds(lag0, n_lags)], out_ref.at[:, pl.ds(lag0, n_lags)], out_sem.at[slot])

        def body(i, carry):
            b, h = i // 2, i % 2
            piece(i * half, half, pl.multiple_of(h * (half * rows), half * rows),
                  pl.multiple_of(b * FINE, FINE))
            if last:
                send(i * half, half, i).start()
            return carry

        lax.fori_loop(0, 2 * coarse, body, 0)
        piece(coarse * FINE, 1, 0, coarse * FINE)
        if last:
            send(coarse * FINE, 1, 2 * coarse).start()
            for i in range(2 * coarse):
                send(i * half, half, i).wait()
            send(coarse * FINE, 1, 2 * coarse).wait()

    for h in range(n_parts):
        prepare(h)
    tail = n_parts - 1
    for h in range(tail):
        for k in range(n_chunks):
            forward(0, k, h)
    early = n_shift // 2
    for i in range(early):
        shift_part(i)
    delay = max(2, n_shift - early - 1)
    for turn in range(n_chunks + delay):
        if turn < n_chunks:
            forward(0, turn, tail)
            for h in range(tail):
                forward(1, turn, h)
        if 0 <= turn - 1 < n_chunks:
            forward(1, turn - 1, tail)
        if early + turn < n_shift:
            shift_part(early + turn)
        if turn - delay >= 0:
            correlate(turn - delay)

    for copy in raw_copies + z_copies + y_copies:
        copy.wait_send()


def on_device(n_ta, n_ch, raw_strain, band_index, filter_taps):
    block, length = raw_strain.shape
    rows = block // n_ta
    whole = n_ta * length
    chunk = length // SUBS
    n_chunks = n_ta * SUBS
    n_parts = max(1, min(PARTS, rows // 16))
    tall = block // n_parts
    dma = pltpu.SemaphoreType.DMA
    return pl.pallas_call(
        functools.partial(kernel, n_ta, n_ch, rows, length, n_parts),
        out_shape=jax.ShapeDtypeStruct((ROUNDS, LAGS, rows, block), F32),
        in_specs=[
            pl.BlockSpec(memory_space=pltpu.HBM),
            pl.BlockSpec(memory_space=pltpu.HBM),
            pl.BlockSpec(memory_space=pltpu.HBM),
        ],
        out_specs=pl.BlockSpec(memory_space=pl.ANY),
        scratch_shapes=[
            pltpu.VMEM((1, block), jnp.int32),
            pltpu.SMEM((NBANDS, TAPS), F32),
            pltpu.VMEM((n_parts, tall, length), F32),
            pltpu.VMEM((tall, length + 256), F32),
            pltpu.VMEM((tall, length), F32),
            pltpu.VMEM((tall, length), F32),
            pltpu.VMEM((tall, length), F32),
            pltpu.VMEM((n_chunks, rows, chunk), BF16),
            pltpu.VMEM((rows, whole + PADK), BF16),
            pltpu.VMEM((FINE * rows, whole + PADK), BF16),
            pltpu.VMEM((ROUNDS, n_chunks, block, chunk), BF16),
            pltpu.VMEM((2 * LAGH + whole + PADK, ROUNDS * block), BF16),
            pltpu.VMEM((ROUNDS, LAGS, rows, block), F32),
            pltpu.VMEM((256, NBANDS * 128), BF16),
            pltpu.VMEM((256, NBANDS * 128), BF16),
            pltpu.VMEM((256, 512), BF16),
            pltpu.VMEM((length // 128 * tall, 256), BF16),
            pltpu.VMEM((length // 128 * tall, 256), BF16),
            dma((2,)),
            dma((n_parts,)),
            dma((n_parts, n_ta)),
            dma((n_parts, n_ta)),
            dma((ROUNDS, n_chunks, n_parts)),
            dma((ROUNDS, n_chunks, n_parts, n_ta)),
            dma((ROUNDS, n_chunks, n_parts, n_ta)),
            dma((2 * (LAGS // FINE) + 1,)),
        ],
        compiler_params=pltpu.CompilerParams(
            collective_id=0, has_side_effects=True, vmem_limit_bytes=32 * 1024 * 1024),
    )(raw_strain, band_index.reshape(1, block), filter_taps)


def solution(mesh):
    placed = (P("ch", "ta"), P("ch"), P())
    return jax.shard_map(
        functools.partial(on_device, mesh.shape["ta"], mesh.shape["ch"]),
        mesh=mesh,
        in_specs=placed,
        out_specs=P(None, None, ("ch", "ta"), None),
        check_vma=False,
    )
```

```python
import functools
import math

import jax
import jax.numpy as jnp
from jax import lax
from jax.experimental import pallas as pl
from jax.experimental.pallas import tpu as pltpu
from jax.sharding import PartitionSpec as P

HF = 16
TAPS = 33
NBANDS = 4
LAGH = 32
LAGS = 65
ROUNDS = 2
FINE = 16
SUBS = 2
PARTS = 2
PADK = 128
MESH = pl.DeviceIdType.MESH
F32 = jnp.float32
BF16 = jnp.bfloat16


def split(x):
    high = x.astype(BF16)
    return high, (x - high.astype(F32)).astype(BF16)


def dot(a, b):
    return jnp.dot(a, b, preferred_element_type=F32)


def kernel(n_ta, n_ch, rows, length, n_parts, raw_ref, band_hbm, taps_hbm, acc,
           band_ref, taps_ref, x, xe, f, pre, suf, nbuf, own, shifted, qbuf, pt, w_hi, w_lo, tri, xs_hi, xs_lo,
           small_sem, local_sem, raw_send, raw_recv, z_send, q_recv, y_send):
    a = lax.axis_index("ta")
    c = lax.axis_index("ch")
    off = n_ch // 4
    up = lax.rem(c + off, n_ch)
    down = lax.rem(c + n_ch - off, n_ch)
    whole = n_ta * length
    block = n_ta * rows
    hr = rows // n_parts
    tall = n_ta * hr
    chunk = length // SUBS
    n_chunks = n_ta * SUBS
    others = range(1, n_ta)

    def peer(p):
        return lax.rem(a + p, n_ta)

    def source(p):
        return lax.rem(a + n_ta - p, n_ta)

    def rows_of(g, h):
        return pl.ds(pl.multiple_of(g * rows + h * hr, hr), hr)

    def place(g):
        return pl.ds(pl.multiple_of(g * hr, hr), hr)

    small = [pltpu.make_async_copy(band_hbm, band_ref, small_sem.at[0]),
             pltpu.make_async_copy(taps_hbm, taps_ref, small_sem.at[1])]
    mine = [pltpu.make_async_copy(raw_ref.at[rows_of(a, h)], x.at[h, place(a)], local_sem.at[h])
            for h in range(n_parts)]
    for copy in small + mine:
        copy.start()

    barrier = pltpu.get_barrier_semaphore()
    for target in (up, down):
        pl.semaphore_signal(barrier, inc=1, device_id=(target, a), device_id_type=MESH)
    for p in others:
        pl.semaphore_signal(barrier, inc=1, device_id=(c, peer(p)), device_id_type=MESH)
    pl.semaphore_wait(barrier, 2 + len(others))

    raw_copies = []
    for h in range(n_parts):
        for p in others:
            copy = pltpu.make_async_remote_copy(
                src_ref=raw_ref.at[rows_of(peer(p), h)], dst_ref=x.at[h, place(a)],
                send_sem=raw_send.at[h, p], recv_sem=raw_recv.at[h, p],
                device_id=(c, peer(p)), device_id_type=MESH)
            copy.start()
            raw_copies.append(copy)
    for copy in small:
        copy.wait()

    used = 160
    lane = lax.broadcasted_iota(jnp.int32, (used, 128), 1)
    row = lax.broadcasted_iota(jnp.int32, (used, 128), 0)
    diff = row - lane
    for b in range(NBANDS):
        w = jnp.zeros((used, 128), F32)
        for k in range(TAPS):
            w = jnp.where(diff == k, taps_ref[b, k], w)
        high, low = split(w)
        cols = slice(b * 128, (b + 1) * 128)
        w_hi[0:used, cols] = high
        w_lo[0:used, cols] = low
        w_hi[used:256, cols] = jnp.zeros((256 - used, 128), BF16)
        w_lo[used:256, cols] = jnp.zeros((256 - used, 128), BF16)
    r256 = lax.broadcasted_iota(jnp.int32, (256, 256), 0)
    c256 = lax.broadcasted_iota(jnp.int32, (256, 256), 1)
    tri[:, 0:256] = jnp.where(r256 <= c256, 1.0, 0.0).astype(BF16)
    tri[:, 256:512] = jnp.where(r256 >= c256, 1.0, 0.0).astype(BF16)
    pt[0:2 * LAGH, :] = jnp.zeros((2 * LAGH, ROUNDS * block), BF16)
    pt[2 * LAGH + whole:, :] = jnp.zeros((pt.shape[0] - 2 * LAGH - whole, ROUNDS * block), BF16)
    own[:, whole:] = jnp.zeros((rows, PADK), BF16)

    z_copies = []

    def prepare(h):
        row = lax.broadcasted_iota(jnp.int32, (tall, block), 0)
        chosen = lax.broadcasted_iota(jnp.int32, (tall, block), 1) == a * rows + h * hr + lax.rem(row, hr)
        bands = jnp.sum(jnp.where(chosen, band_ref[...].astype(F32), 0.0), axis=1, keepdims=True)
        bands = jnp.broadcast_to(bands, (tall, 128))

        mine[h].wait()
        for p in others:
            slot = x.at[h, place(source(p))]
            pltpu.make_async_remote_copy(
                src_ref=slot, dst_ref=slot,
                send_sem=raw_send.at[h, p], recv_sem=raw_recv.at[h, p],
                device_id=(c, source(p)), device_id_type=MESH).wait_recv()

        xe[:, 128:128 + length] = x[h]
        zeros = jnp.zeros((hr, 128), F32)
        for g in range(n_ta):
            here = slice(g * hr, (g + 1) * hr)
            xe[here, 0:128] = x[h, (g - 1) * hr:g * hr, length - 128:] if g > 0 else zeros
            xe[here, 128 + length:] = x[h, (g + 1) * hr:(g + 2) * hr, 0:128] if g < n_ta - 1 else zeros
        moved = pltpu.roll(xe[...], 128 + length + 128 - (128 - HF), 1)
        x_hi, x_lo = split(moved)
        for n in range(length // 128):
            lanes = slice(128 * n, 128 * n + 256)
            xs_hi[n * tall:(n + 1) * tall, :] = x_hi[:, lanes]
            xs_lo[n * tall:(n + 1) * tall, :] = x_lo[:, lanes]
        for m in range(length // 512):
            part = slice(4 * m * tall, 4 * (m + 1) * tall)
            res = dot(xs_hi[part, :], w_hi[...]) + (dot(xs_lo[part, :], w_hi[...]) + dot(xs_hi[part, :], w_lo[...]))
            for q in range(4):
                one = res[q * tall:(q + 1) * tall]
                picked = one[:, 0:128]
                for b in range(1, NBANDS):
                    picked = jnp.where(bands == float(b), one[:, b * 128:(b + 1) * 128], picked)
                f[:, 128 * (4 * m + q):128 * (4 * m + q + 1)] = picked

        pending = [k for k in range(n_chunks) if h > 0]
        for k in pending[:n_chunks // 4]:
            forward(0, k, h - 1)

        n_sum = length // 256
        total = jnp.zeros((tall, 1), F32)
        totals = []
        for m in range(n_sum):
            lanes = slice(256 * m, 256 * (m + 1))
            high, low = split(jnp.abs(f[:, lanes]))
            res = dot(high, tri[...]) + dot(low, tri[...])
            pre[:, lanes] = res[:, 0:256] + total
            suf[:, lanes] = res[:, 256:512]
            part = res[:, 255:256]
            totals.append(part)
            total = total + part
        behind = jnp.zeros((tall, 1), F32)
        for m in reversed(range(n_sum)):
            lanes = slice(256 * m, 256 * (m + 1))
            if m < n_sum - 1:
                behind = behind + totals[m + 1]
                suf[:, lanes] = suf[:, lanes] + behind

        for k in pending[n_chunks // 4:n_chunks // 2]:
            forward(0, k, h - 1)

        ours = slice(h * hr, (h + 1) * hr)
        for k in range(n_chunks):
            g, s = k // SUBS, k % SUBS
            lanes = slice(s * chunk, (s + 1) * chunk)
            here = slice(g * hr, (g + 1) * hr)
            window = jnp.broadcast_to(total[here], (hr, chunk))
            if g > 0:
                window = window + suf[(g - 1) * hr:g * hr, lanes]
            if g < n_ta - 1:
                window = window + pre[(g + 1) * hr:(g + 2) * hr, lanes]
            time = k * chunk + lax.broadcasted_iota(jnp.int32, (1, chunk), 1)
            counted = jnp.minimum(time + length, whole - 1) + 1 - jnp.maximum(time - length, 0)
            level = window * (1.0 / counted.astype(F32))
            normalized = (f[here, lanes] / (level + 1e-6)).astype(BF16)
            nbuf[k, ours] = normalized
            own[ours, k * chunk:(k + 1) * chunk] = normalized
            copy = pltpu.make_async_remote_copy(
                src_ref=nbuf.at[k, ours], dst_ref=qbuf.at[0, k, rows_of(a, h)],
                send_sem=z_send.at[0, k, h], recv_sem=q_recv.at[0, k, h, 0],
                device_id=(up, a), device_id_type=MESH)
            copy.start()
            z_copies.append(copy)
        for k in pending[n_chunks // 2:]:
            forward(0, k, h - 1)

    step = min(rows, 16)
    n_shift = rows // step

    def shift_part(i):
        part = own[i * step:(i + 1) * step, :]
        for fine in range(FINE):
            shifted[fine * rows + i * step:fine * rows + (i + 1) * step, :] = (
                pltpu.roll(part, LAGH + fine, 1).astype(BF16))

    y_copies = []

    def arrived(r, k, h, p):
        slot = qbuf.at[r, k, rows_of(source(p), h)]
        pltpu.make_async_remote_copy(
            src_ref=slot, dst_ref=slot, send_sem=z_send.at[0, k, h], recv_sem=q_recv.at[r, k, h, p],
            device_id=(c, a), device_id_type=MESH).wait_recv()

    def forward(r, k, h):
        arrived(r, k, h, 0)
        slot = (r, k, rows_of(a, h))
        if r + 1 < ROUNDS:
            copy = pltpu.make_async_remote_copy(
                src_ref=qbuf.at[slot], dst_ref=qbuf.at[r + 1, k, rows_of(a, h)],
                send_sem=z_send.at[r + 1, k, h], recv_sem=q_recv.at[r + 1, k, h, 0],
                device_id=(up, a), device_id_type=MESH)
            copy.start()
            z_copies.append(copy)
        for p in others:
            copy = pltpu.make_async_remote_copy(
                src_ref=qbuf.at[slot], dst_ref=qbuf.at[slot],
                send_sem=y_send.at[r, k, h, p], recv_sem=q_recv.at[r, k, h, p],
                device_id=(c, peer(p)), device_id_type=MESH)
            copy.start()
            y_copies.append(copy)

    scale = 1.0 / math.sqrt(whole)
    half = FINE // 2
    coarse = LAGS // FINE

    def correlate(k):
        for r in range(ROUNDS):
            for h in range(n_parts):
                for p in others:
                    arrived(r, k, h, p)
            pt[2 * LAGH + k * chunk:2 * LAGH + (k + 1) * chunk, r * block:(r + 1) * block] = qbuf[r, k].T
        first, last = k == 0, k == n_chunks - 1
        begin = k * chunk
        depth = chunk + (PADK if last else 0)

        def piece(lag0, n_lags, row0, shift):
            res = dot(shifted[pl.ds(row0, n_lags * rows), begin:begin + depth],
                      pt[pl.ds(begin + shift, depth), :])
            for r in range(ROUNDS):
                part = res[:, r * block:(r + 1) * block].reshape(n_lags, rows, block)
                where = (r, pl.ds(lag0, n_lags))
                if not first:
                    part = acc[where] + part
                acc[where] = part * scale if last else part

        def body(i, carry):
            b, h = i // 2, i % 2
            piece(i * half, half, pl.multiple_of(h * (half * rows), half * rows),
                  pl.multiple_of(b * FINE, FINE))
            return carry

        lax.fori_loop(0, 2 * coarse, body, 0)
        piece(coarse * FINE, 1, 0, coarse * FINE)

    for h in range(n_parts):
        prepare(h)
    tail = n_parts - 1
    early = n_shift // 2
    for i in range(early):
        shift_part(i)
    delay = max(2, n_shift - early - 1)
    for turn in range(n_chunks + delay):
        if turn < n_chunks:
            forward(0, turn, tail)
            for h in range(tail):
                forward(1, turn, h)
        if 0 <= turn - 1 < n_chunks:
            forward(1, turn - 1, tail)
        if early + turn < n_shift:
            shift_part(early + turn)
        if turn - delay >= 0:
            correlate(turn - delay)

    for copy in raw_copies + z_copies + y_copies:
        copy.wait_send()


def on_device(n_ta, n_ch, raw_strain, band_index, filter_taps):
    block, length = raw_strain.shape
    rows = block // n_ta
    whole = n_ta * length
    chunk = length // SUBS
    n_chunks = n_ta * SUBS
    n_parts = max(1, min(PARTS, rows // 16))
    tall = block // n_parts
    dma = pltpu.SemaphoreType.DMA
    return pl.pallas_call(
        functools.partial(kernel, n_ta, n_ch, rows, length, n_parts),
        out_shape=jax.ShapeDtypeStruct((ROUNDS, LAGS, rows, block), F32),
        in_specs=[
            pl.BlockSpec(memory_space=pltpu.HBM),
            pl.BlockSpec(memory_space=pltpu.HBM),
            pl.BlockSpec(memory_space=pltpu.HBM),
        ],
        out_specs=pl.BlockSpec(memory_space=pltpu.VMEM),
        scratch_shapes=[
            pltpu.VMEM((1, block), jnp.int32),
            pltpu.SMEM((NBANDS, TAPS), F32),
            pltpu.VMEM((n_parts, tall, length), F32),
            pltpu.VMEM((tall, length + 256), F32),
            pltpu.VMEM((tall, length), F32),
            pltpu.VMEM((tall, length), F32),
            pltpu.VMEM((tall, length), F32),
            pltpu.VMEM((n_chunks, rows, chunk), BF16),
            pltpu.VMEM((rows, whole + PADK), BF16),
            pltpu.VMEM((FINE * rows, whole + PADK), BF16),
            pltpu.VMEM((ROUNDS, n_chunks, block, chunk), BF16),
            pltpu.VMEM((2 * LAGH + whole + PADK, ROUNDS * block), BF16),
            pltpu.VMEM((256, NBANDS * 128), BF16),
            pltpu.VMEM((256, NBANDS * 128), BF16),
            pltpu.VMEM((256, 512), BF16),
            pltpu.VMEM((length // 128 * tall, 256), BF16),
            pltpu.VMEM((length // 128 * tall, 256), BF16),
            dma((2,)),
            dma((n_parts,)),
            dma((n_parts, n_ta)),
            dma((n_parts, n_ta)),
            dma((ROUNDS, n_chunks, n_parts)),
            dma((ROUNDS, n_chunks, n_parts, n_ta)),
            dma((ROUNDS, n_chunks, n_parts, n_ta)),
        ],
        compiler_params=pltpu.CompilerParams(
            collective_id=0, has_side_effects=True, vmem_limit_bytes=32 * 1024 * 1024),
    )(raw_strain, band_index.reshape(1, block), filter_taps)


def solution(mesh):
    placed = (P("ch", "ta"), P("ch"), P())
    return jax.shard_map(
        functools.partial(on_device, mesh.shape["ta"], mesh.shape["ch"]),
        mesh=mesh,
        in_specs=placed,
        out_specs=P(None, None, ("ch", "ta"), None),
        check_vma=False,
    )
```

```python
import functools
import math

import jax
import jax.numpy as jnp
from jax import lax
from jax.experimental import pallas as pl
from jax.experimental.pallas import tpu as pltpu
from jax.sharding import PartitionSpec as P

HF = 16
TAPS = 33
NBANDS = 4
LAGH = 32
LAGS = 65
ROUNDS = 2
FINE = 16
SUBS = 3
PARTS = 2
PADK = 128
MESH = pl.DeviceIdType.MESH
F32 = jnp.float32
BF16 = jnp.bfloat16


def split(x):
    high = x.astype(BF16)
    return high, (x - high.astype(F32)).astype(BF16)


def dot(a, b):
    return jnp.dot(a, b, preferred_element_type=F32)


def kernel(n_ta, n_ch, rows, length, n_parts, raw_ref, band_hbm, taps_hbm, acc,
           band_ref, taps_ref, x, xe, f, pre, suf, nbuf, own, shifted, qbuf, pt, w_hi, w_lo, tri, xs_hi, xs_lo,
           small_sem, local_sem, raw_send, raw_recv, z_send, q_recv, y_send):
    a = lax.axis_index("ta")
    c = lax.axis_index("ch")
    off = n_ch // 4
    up = lax.rem(c + off, n_ch)
    down = lax.rem(c + n_ch - off, n_ch)
    whole = n_ta * length
    block = n_ta * rows
    hr = rows // n_parts
    tall = n_ta * hr
    chunk = length // SUBS
    n_chunks = n_ta * SUBS
    others = range(1, n_ta)

    def peer(p):
        return lax.rem(a + p, n_ta)

    def source(p):
        return lax.rem(a + n_ta - p, n_ta)

    def rows_of(g, h):
        return pl.ds(pl.multiple_of(g * rows + h * hr, hr), hr)

    def place(g):
        return pl.ds(pl.multiple_of(g * hr, hr), hr)

    small = [pltpu.make_async_copy(band_hbm, band_ref, small_sem.at[0]),
             pltpu.make_async_copy(taps_hbm, taps_ref, small_sem.at[1])]
    mine = [pltpu.make_async_copy(raw_ref.at[rows_of(a, h)], x.at[h, place(a)], local_sem.at[h])
            for h in range(n_parts)]
    for copy in small + mine:
        copy.start()

    barrier = pltpu.get_barrier_semaphore()
    for target in (up, down):
        pl.semaphore_signal(barrier, inc=1, device_id=(target, a), device_id_type=MESH)
    for p in others:
        pl.semaphore_signal(barrier, inc=1, device_id=(c, peer(p)), device_id_type=MESH)
    pl.semaphore_wait(barrier, 2 + len(others))

    raw_copies = []
    for h in range(n_parts):
        for p in others:
            copy = pltpu.make_async_remote_copy(
                src_ref=raw_ref.at[rows_of(peer(p), h)], dst_ref=x.at[h, place(a)],
                send_sem=raw_send.at[h, p], recv_sem=raw_recv.at[h, p],
                device_id=(c, peer(p)), device_id_type=MESH)
            copy.start()
            raw_copies.append(copy)
    for copy in small:
        copy.wait()

    used = 160
    lane = lax.broadcasted_iota(jnp.int32, (used, 128), 1)
    row = lax.broadcasted_iota(jnp.int32, (used, 128), 0)
    diff = row - lane
    for b in range(NBANDS):
        w = jnp.zeros((used, 128), F32)
        for k in range(TAPS):
            w = jnp.where(diff == k, taps_ref[b, k], w)
        high, low = split(w)
        cols = slice(b * 128, (b + 1) * 128)
        w_hi[0:used, cols] = high
        w_lo[0:used, cols] = low
        w_hi[used:256, cols] = jnp.zeros((256 - used, 128), BF16)
        w_lo[used:256, cols] = jnp.zeros((256 - used, 128), BF16)
    r256 = lax.broadcasted_iota(jnp.int32, (256, 256), 0)
    c256 = lax.broadcasted_iota(jnp.int32, (256, 256), 1)
    tri[:, 0:256] = jnp.where(r256 <= c256, 1.0, 0.0).astype(BF16)
    tri[:, 256:512] = jnp.where(r256 >= c256, 1.0, 0.0).astype(BF16)
    pt[0:2 * LAGH, :] = jnp.zeros((2 * LAGH, ROUNDS * block), BF16)
    pt[2 * LAGH + whole:, :] = jnp.zeros((pt.shape[0] - 2 * LAGH - whole, ROUNDS * block), BF16)
    own[:, whole:] = jnp.zeros((rows, PADK), BF16)

    z_copies = []

    def prepare(h):
        row = lax.broadcasted_iota(jnp.int32, (tall, block), 0)
        chosen = lax.broadcasted_iota(jnp.int32, (tall, block), 1) == a * rows + h * hr + lax.rem(row, hr)
        bands = jnp.sum(jnp.where(chosen, band_ref[...].astype(F32), 0.0), axis=1, keepdims=True)
        bands = jnp.broadcast_to(bands, (tall, 128))

        mine[h].wait()
        for p in others:
            slot = x.at[h, place(source(p))]
            pltpu.make_async_remote_copy(
                src_ref=slot, dst_ref=slot,
                send_sem=raw_send.at[h, p], recv_sem=raw_recv.at[h, p],
                device_id=(c, source(p)), device_id_type=MESH).wait_recv()

        xe[:, 128:128 + length] = x[h]
        zeros = jnp.zeros((hr, 128), F32)
        for g in range(n_ta):
            here = slice(g * hr, (g + 1) * hr)
            xe[here, 0:128] = x[h, (g - 1) * hr:g * hr, length - 128:] if g > 0 else zeros
            xe[here, 128 + length:] = x[h, (g + 1) * hr:(g + 2) * hr, 0:128] if g < n_ta - 1 else zeros
        moved = pltpu.roll(xe[...], 128 + length + 128 - (128 - HF), 1)
        x_hi, x_lo = split(moved)
        for n in range(length // 128):
            lanes = slice(128 * n, 128 * n + 256)
            xs_hi[n * tall:(n + 1) * tall, :] = x_hi[:, lanes]
            xs_lo[n * tall:(n + 1) * tall, :] = x_lo[:, lanes]
        for m in range(length // 512):
            part = slice(4 * m * tall, 4 * (m + 1) * tall)
            res = dot(xs_hi[part, :], w_hi[...]) + (dot(xs_lo[part, :], w_hi[...]) + dot(xs_hi[part, :], w_lo[...]))
            for q in range(4):
                one = res[q * tall:(q + 1) * tall]
                picked = one[:, 0:128]
                for b in range(1, NBANDS):
                    picked = jnp.where(bands == float(b), one[:, b * 128:(b + 1) * 128], picked)
                f[:, 128 * (4 * m + q):128 * (4 * m + q + 1)] = picked

        pending = [k for k in range(n_chunks) if h > 0]
        for k in pending[:n_chunks // 4]:
            forward(0, k, h - 1)

        n_sum = length // 256
        total = jnp.zeros((tall, 1), F32)
        totals = []
        for m in range(n_sum):
            lanes = slice(256 * m, 256 * (m + 1))
            high, low = split(jnp.abs(f[:, lanes]))
            res = dot(high, tri[...]) + dot(low, tri[...])
            pre[:, lanes] = res[:, 0:256] + total
            suf[:, lanes] = res[:, 256:512]
            part = res[:, 255:256]
            totals.append(part)
            total = total + part
        behind = jnp.zeros((tall, 1), F32)
        for m in reversed(range(n_sum)):
            lanes = slice(256 * m, 256 * (m + 1))
            if m < n_sum - 1:
                behind = behind + totals[m + 1]
                suf[:, lanes] = suf[:, lanes] + behind

        for k in pending[n_chunks // 4:n_chunks // 2]:
            forward(0, k, h - 1)

        ours = slice(h * hr, (h + 1) * hr)
        for k in range(n_chunks):
            g, s = k // SUBS, k % SUBS
            lanes = slice(s * chunk, (s + 1) * chunk)
            here = slice(g * hr, (g + 1) * hr)
            window = jnp.broadcast_to(total[here], (hr, chunk))
            if g > 0:
                window = window + suf[(g - 1) * hr:g * hr, lanes]
            if g < n_ta - 1:
                window = window + pre[(g + 1) * hr:(g + 2) * hr, lanes]
            time = k * chunk + lax.broadcasted_iota(jnp.int32, (1, chunk), 1)
            counted = jnp.minimum(time + length, whole - 1) + 1 - jnp.maximum(time - length, 0)
            level = window * (1.0 / counted.astype(F32))
            normalized = (f[here, lanes] / (level + 1e-6)).astype(BF16)
            nbuf[k, ours] = normalized
            own[ours, k * chunk:(k + 1) * chunk] = normalized
            copy = pltpu.make_async_remote_copy(
                src_ref=nbuf.at[k, ours], dst_ref=qbuf.at[0, k, rows_of(a, h)],
                send_sem=z_send.at[0, k, h], recv_sem=q_recv.at[0, k, h, 0],
                device_id=(up, a), device_id_type=MESH)
            copy.start()
            z_copies.append(copy)
        for k in pending[n_chunks // 2:]:
            forward(0, k, h - 1)

    step = min(rows, 16)
    n_shift = rows // step

    def shift_part(i):
        part = own[i * step:(i + 1) * step, :]
        for fine in range(FINE):
            shifted[fine * rows + i * step:fine * rows + (i + 1) * step, :] = (
                pltpu.roll(part, LAGH + fine, 1).astype(BF16))

    y_copies = []

    def arrived(r, k, h, p):
        slot = qbuf.at[r, k, rows_of(source(p), h)]
        pltpu.make_async_remote_copy(
            src_ref=slot, dst_ref=slot, send_sem=z_send.at[0, k, h], recv_sem=q_recv.at[r, k, h, p],
            device_id=(c, a), device_id_type=MESH).wait_recv()

    def forward(r, k, h):
        arrived(r, k, h, 0)
        slot = (r, k, rows_of(a, h))
        if r + 1 < ROUNDS:
            copy = pltpu.make_async_remote_copy(
                src_ref=qbuf.at[slot], dst_ref=qbuf.at[r + 1, k, rows_of(a, h)],
                send_sem=z_send.at[r + 1, k, h], recv_sem=q_recv.at[r + 1, k, h, 0],
                device_id=(up, a), device_id_type=MESH)
            copy.start()
            z_copies.append(copy)
        for p in others:
            copy = pltpu.make_async_remote_copy(
                src_ref=qbuf.at[slot], dst_ref=qbuf.at[slot],
                send_sem=y_send.at[r, k, h, p], recv_sem=q_recv.at[r, k, h, p],
                device_id=(c, peer(p)), device_id_type=MESH)
            copy.start()
            y_copies.append(copy)

    scale = 1.0 / math.sqrt(whole)
    half = FINE // 2
    coarse = LAGS // FINE

    def correlate(k):
        for r in range(ROUNDS):
            for h in range(n_parts):
                for p in others:
                    arrived(r, k, h, p)
            pt[2 * LAGH + k * chunk:2 * LAGH + (k + 1) * chunk, r * block:(r + 1) * block] = qbuf[r, k].T
        first, last = k == 0, k == n_chunks - 1
        begin = k * chunk
        depth = chunk + (PADK if last else 0)

        def piece(lag0, n_lags, row0, shift):
            res = dot(shifted[pl.ds(row0, n_lags * rows), begin:begin + depth],
                      pt[pl.ds(begin + shift, depth), :])
            for r in range(ROUNDS):
                part = res[:, r * block:(r + 1) * block].reshape(n_lags, rows, block)
                where = (r, pl.ds(lag0, n_lags))
                if not first:
                    part = acc[where] + part
                acc[where] = part * scale if last else part

        def body(i, carry):
            b, h = i // 2, i % 2
            piece(i * half, half, pl.multiple_of(h * (half * rows), half * rows),
                  pl.multiple_of(b * FINE, FINE))
            return carry

        lax.fori_loop(0, 2 * coarse, body, 0)
        piece(coarse * FINE, 1, 0, coarse * FINE)

    for h in range(n_parts):
        prepare(h)
    tail = n_parts - 1
    early = n_shift // 2
    for i in range(early):
        shift_part(i)
    delay = max(2, n_shift - early - 1)
    for turn in range(n_chunks + delay):
        if turn < n_chunks:
            forward(0, turn, tail)
            for h in range(tail):
                forward(1, turn, h)
        if 0 <= turn - 1 < n_chunks:
            forward(1, turn - 1, tail)
        if early + turn < n_shift:
            shift_part(early + turn)
        if turn - delay >= 0:
            correlate(turn - delay)

    for copy in raw_copies + z_copies + y_copies:
        copy.wait_send()


def on_device(n_ta, n_ch, raw_strain, band_index, filter_taps):
    block, length = raw_strain.shape
    rows = block // n_ta
    whole = n_ta * length
    chunk = length // SUBS
    n_chunks = n_ta * SUBS
    n_parts = max(1, min(PARTS, rows // 16))
    tall = block // n_parts
    dma = pltpu.SemaphoreType.DMA
    return pl.pallas_call(
        functools.partial(kernel, n_ta, n_ch, rows, length, n_parts),
        out_shape=jax.ShapeDtypeStruct((ROUNDS, LAGS, rows, block), F32),
        in_specs=[
            pl.BlockSpec(memory_space=pltpu.HBM),
            pl.BlockSpec(memory_space=pltpu.HBM),
            pl.BlockSpec(memory_space=pltpu.HBM),
        ],
        out_specs=pl.BlockSpec(memory_space=pltpu.VMEM),
        scratch_shapes=[
            pltpu.VMEM((1, block), jnp.int32),
            pltpu.SMEM((NBANDS, TAPS), F32),
            pltpu.VMEM((n_parts, tall, length), F32),
            pltpu.VMEM((tall, length + 256), F32),
            pltpu.VMEM((tall, length), F32),
            pltpu.VMEM((tall, length), F32),
            pltpu.VMEM((tall, length), F32),
            pltpu.VMEM((n_chunks, rows, chunk), BF16),
            pltpu.VMEM((rows, whole + PADK), BF16),
            pltpu.VMEM((FINE * rows, whole + PADK), BF16),
            pltpu.VMEM((ROUNDS, n_chunks, block, chunk), BF16),
            pltpu.VMEM((2 * LAGH + whole + PADK, ROUNDS * block), BF16),
            pltpu.VMEM((256, NBANDS * 128), BF16),
            pltpu.VMEM((256, NBANDS * 128), BF16),
            pltpu.VMEM((256, 512), BF16),
            pltpu.VMEM((length // 128 * tall, 256), BF16),
            pltpu.VMEM((length // 128 * tall, 256), BF16),
            dma((2,)),
            dma((n_parts,)),
            dma((n_parts, n_ta)),
            dma((n_parts, n_ta)),
            dma((ROUNDS, n_chunks, n_parts)),
            dma((ROUNDS, n_chunks, n_parts, n_ta)),
            dma((ROUNDS, n_chunks, n_parts, n_ta)),
        ],
        compiler_params=pltpu.CompilerParams(
            collective_id=0, has_side_effects=True, vmem_limit_bytes=32 * 1024 * 1024),
    )(raw_strain, band_index.reshape(1, block), filter_taps)


def solution(mesh):
    placed = (P("ch", "ta"), P("ch"), P())
    return jax.shard_map(
        functools.partial(on_device, mesh.shape["ta"], mesh.shape["ch"]),
        mesh=mesh,
        in_specs=placed,
        out_specs=P(None, None, ("ch", "ta"), None),
        check_vma=False,
    )
```
